32 devices in a mesh: groups: 2 (over y), wide: 4 (over z), narrow: 4 (over x, core).
Axes of the slice: x: 2, y: 2, z: 4, core: 2. Of those that a mesh axis runs over, the one named last changes fastest.
Arguments:
- tokens: bfloat16 [1536, 8192], P(('groups', 'wide'), 'narrow'), parts along dimension 0, may hold values from -6 to 6
- tenant_ids: int32 [768], P('wide'), may hold values from 0 to 1, as said below
- placement: int32 [4], replicated, may hold values from 0 to 1, as said below
- base_weight: bfloat16 [8192, 512], P(None, 'narrow'), may hold values from -0.0625 to 0.0625
- delta_levels: bfloat16 [4, 8192, 512], P('wide', None, 'narrow'), may hold values from -8 to 7, as said below
- delta_scales: float32 [4, 512], P('wide', 'narrow'), may hold values from 0.0005 to 0.002
- outlier_index: int32 [4, 128], P('wide'), may hold values from 0 to 8191, as said below
- outlier_values: bfloat16 [4, 128, 512], P('wide', None, 'narrow'), may hold values from -0.125 to 0.125
Outputs:
- adapted_out: bfloat16 [1536, 512], P(('groups', 'wide'), 'narrow'), parts along dimension 0
The draws below stay inside these ranges and needn't reach their ends.
There are 2 independent parts, one for each index of `groups`. The reference program is written for one: setup_inputs(seed, part) draws one part's arguments, and reference() takes and returns one part's arrays. A program takes and returns all parts, laid end to end along the dimension named above; an argument that names none is the same for every part. Nothing has to cross between parts.
Inputs may be any that keep to these rules, and one draw needn't show every extreme that they name: `placement`: every tenant 0 to 1 is held by at least one index; several indices may hold the same tenant. `tenant_ids`: among the 192 rows of one index of wide, at most 120 name the same tenant, and in every such block some tenant is named by exactly 120 rows. `delta_levels`: whole numbers. Indices with equal placement entries hold equal delta_levels, delta_scales, outlier_index and outlier_values. `outlier_index`: each holder's list names 128 distinct features, among them feature 0 and feature 8192 - 1.
All inputs are finite; a program needn't handle non-finite values.
Results may differ from the reference program's by a relative error of at most 0.0039.
Values may be sent and summed in bfloat16 or wider, within the bound.
A program may use at most 128 MiB of HBM per device.

```python
import jax
import jax.numpy as jnp
from jax import lax

D = 8192
K_OUT = 128
ROWS_DEV = 192
ROWS = 768
FF = 512
TENANTS = 2
CAP = 120
N_WIDE = 4


def tenant_layout(key):
    order = jax.random.permutation(jax.random.fold_in(key, 101), TENANTS).astype(jnp.int32)
    hot_count = min(4, TENANTS)
    extra_rank = jax.random.randint(jax.random.fold_in(key, 102), (N_WIDE - TENANTS,), 0, hot_count)
    ranks = jnp.concatenate([jnp.arange(TENANTS, dtype=jnp.int32), extra_rank.astype(jnp.int32)])
    shuffle = jax.random.permutation(jax.random.fold_in(key, 103), N_WIDE)
    return (order, order[ranks[shuffle]])


def draw_placement(key, part):
    order, holders = tenant_layout(key)
    return holders


def draw_tenant_ids(key, part):
    order, holders = tenant_layout(key)
    key = jax.random.fold_in(key, 2)
    hot_count = min(4, TENANTS)
    pool = jnp.repeat(jnp.arange(TENANTS, dtype=jnp.int32), CAP)

    def one_block(block_key):
        first_key, second_key, third_key = jax.random.split(block_key, 3)
        full_rank = jax.random.randint(first_key, (), 0, hot_count).astype(jnp.int32)
        shuffled = jax.random.permutation(second_key, pool)
        moved = jnp.argsort((shuffled == full_rank).astype(jnp.int32), stable=True)
        remaining = shuffled[moved][:ROWS_DEV - CAP]
        block = jnp.concatenate([jnp.full((CAP,), full_rank, jnp.int32), remaining])
        return jax.random.permutation(third_key, block)
    block_ranks = jax.vmap(one_block)(jax.random.split(key, N_WIDE))
    return order[block_ranks.reshape(-1)].astype(jnp.int32)


def draw_delta_levels(key, part):
    order, holders = tenant_layout(key)
    key = jax.random.fold_in(key, 3)

    def one_holder(tenant):
        values = jax.random.randint(jax.random.fold_in(key, tenant), (D, FF), -8, 8).astype(jnp.float32)
        return values.astype(jnp.bfloat16)
    return lax.map(one_holder, holders)


def draw_delta_scales(key, part):
    order, holders = tenant_layout(key)
    key = jax.random.fold_in(key, 4)

    def one_holder(tenant):
        return jnp.exp(jax.random.uniform(jax.random.fold_in(key, tenant), (FF,), jnp.float32, jnp.log(0.0005), jnp.log(0.002)))
    return lax.map(one_holder, holders)


def draw_outlier_index(key, part):
    order, holders = tenant_layout(key)
    key = jax.random.fold_in(key, 5)

    def one_holder(tenant):
        tenant_key = jax.random.fold_in(key, tenant)
        inner = jax.random.permutation(jax.random.fold_in(tenant_key, 1), D - 2)[:K_OUT - 2].astype(jnp.int32) + 1
        listed = jnp.concatenate([jnp.array([0, D - 1], jnp.int32), inner])
        return jax.random.permutation(jax.random.fold_in(tenant_key, 2), listed).astype(jnp.int32)
    return lax.map(one_holder, holders)


def draw_outlier_values(key, part):
    order, holders = tenant_layout(key)
    key = jax.random.fold_in(key, 6)

    def one_holder(tenant):
        values = jax.random.normal(jax.random.fold_in(key, tenant), (K_OUT, FF), jnp.float32)
        return (jnp.clip(values, -2.5, 2.5) * 0.05).astype(jnp.bfloat16)
    return lax.map(one_holder, holders)


def block_scale(stream_key, dims, shards, least, top_value):
    loudness, own = 1.0, jax.random.fold_in(stream_key, 6)
    for dim, shards_of in shards:
        heights = jnp.exp(jax.random.uniform(jax.random.fold_in(own, dim), (shards_of,), jnp.float32, least / len(shards), top_value / len(shards)))
        loudness = loudness * jnp.repeat(heights, dims[dim] // shards_of).reshape([-1 if axis == dim else 1 for axis in range(len(dims))])
    return loudness


def noise(key, extent, deviation, bound, cuts=(), kind=jnp.bfloat16):
    level = block_scale(key, extent, cuts, -0.22, 0.18) if cuts else 1.0
    values = jax.random.normal(key, extent, jnp.float32) * deviation * level
    return jnp.minimum(jnp.maximum(values, -bound), bound).astype(kind)


def setup_inputs(seed: int = 0, part: int = 0) -> dict:
    arg_keys = jax.random.split(jax.random.key(seed), 9)
    own_keys = jax.random.split(jax.random.fold_in(arg_keys[8], part), 9)
    return {
        "tokens": noise(own_keys[0], (ROWS, D), 1.0, 6.0, ((0, 4), (1, 4))),
        "tenant_ids": draw_tenant_ids(jax.random.fold_in(arg_keys[8], 71), part),
        "placement": draw_placement(jax.random.fold_in(arg_keys[8], 71), part),
        "base_weight": noise(arg_keys[3], (D, FF), D ** -0.5, 0.0625, ((1, 4),)),
        "delta_levels": draw_delta_levels(jax.random.fold_in(arg_keys[8], 71), part),
        "delta_scales": draw_delta_scales(jax.random.fold_in(arg_keys[8], 71), part),
        "outlier_index": draw_outlier_index(jax.random.fold_in(arg_keys[8], 71), part),
        "outlier_values": draw_outlier_values(jax.random.fold_in(arg_keys[8], 71), part),
    }


def reference(tokens, tenant_ids, placement, base_weight, delta_levels, delta_scales, outlier_index, outlier_values):
    tokens_wide = tokens.astype(jnp.float32)
    base_part = jnp.dot(tokens_wide, base_weight.astype(jnp.float32), preferred_element_type=jnp.float32)
    tenant_list = jnp.arange(TENANTS, dtype=jnp.int32)
    holder = jnp.argmax((placement[None, :] == tenant_list[:, None]).astype(jnp.int32), axis=1).astype(jnp.int32)
    reach = N_WIDE * CAP

    def one_tenant(tenant):
        owner = holder[tenant]
        ordering = jnp.argsort((tenant_ids != tenant).astype(jnp.int32), stable=True)[:reach].astype(jnp.int32)
        chosen_rows = tokens_wide[ordering]
        product = jnp.dot(chosen_rows, delta_levels[owner].astype(jnp.float32), preferred_element_type=jnp.float32)
        product = product * delta_scales[owner][None, :]
        picked = jnp.take(chosen_rows, outlier_index[owner], axis=1)
        product = product + jnp.dot(picked, outlier_values[owner].astype(jnp.float32), preferred_element_type=jnp.float32)
        rounded = product.astype(jnp.bfloat16).astype(jnp.float32)
        valid = tenant_ids[ordering] == tenant
        return ordering, jnp.where(valid[:, None], rounded, jnp.float32(0.0))

    orderings, updates = lax.map(one_tenant, tenant_list)
    total = jnp.zeros((ROWS, FF), jnp.float32).at[orderings.reshape(-1)].add(updates.reshape(-1, FF))
    return (base_part + total).astype(jnp.bfloat16)
```

```python
import functools

import jax
import jax.numpy as jnp
from jax import lax
from jax.experimental import pallas as pl
from jax.experimental.pallas import tpu as pltpu
from jax.sharding import PartitionSpec as P

MESH = pl.DeviceIdType.MESH
PIECES = 8
META = 16


def kernel(
    place, tenants, scales, index, values, tok, base, levels, out,
    x_all, w_all, ext, from_outer, from_inner, to_inner, to_outer, other, other_index,
    acc_a, acc_b, acc_c,
    load_sem, tok_sem,
    outer_recv, inner_recv, y_recv, x_recv, f_recv, c_recv,
    inner_send, outer_send, y_send, x_send, f_send, c_send,
):
    f32, bf16 = jnp.float32, jnp.bfloat16
    rows, cols = out.shape
    depth = base.shape[0]
    keep = values.shape[0]
    piece = x_all.shape[2]
    head = keep // 2 + META
    g = lax.axis_index("groups")
    w = lax.axis_index("wide")
    n = lax.axis_index("narrow")
    n_core = n + 1 - 2 * (n % 2)
    n_x = (n + 2) % 4
    n_far = n_x + 1 - 2 * (n_x % 2)
    low = w // 2 == 0
    at_end = (w == 0) | (w == 3)
    interior = (w == 1) | (w == 2)
    inner = jnp.where(low, w + 1, w - 1)
    outer = jnp.where(interior, jnp.where(low, w - 1, w + 1), w)
    y = 1 - g

    load_levels = pltpu.make_async_copy(levels, w_all.at[:, pl.ds(cols, cols)], load_sem.at[0])
    load_base = pltpu.make_async_copy(base, w_all.at[:, pl.ds(0, cols)], load_sem.at[1])

    def load_tok(j):
        return pltpu.make_async_copy(
            tok.at[:, pl.ds(j * piece, piece)], x_all.at[n * PIECES + j], tok_sem.at[j]
        )

    for j in range(PIECES):
        load_tok(j).start()
    load_levels.start()
    load_base.start()

    barrier = pltpu.get_barrier_semaphore()
    for peer in ({"narrow": n_core}, {"narrow": n_x}, {"groups": y}, {"wide": inner}):
        pl.semaphore_signal(barrier, inc=1, device_id=peer, device_id_type=MESH)

    @pl.when(interior)
    def _():
        pl.semaphore_signal(barrier, inc=1, device_id={"wide": outer}, device_id_type=MESH)

    ext[pl.ds(0, keep // 2), :] = values[pl.ds(pl.multiple_of(g * (keep // 2), keep // 2), keep // 2), :]
    scale = scales[...]
    top = scale.astype(bf16).astype(f32)
    mid = (scale - top).astype(bf16).astype(f32)
    last = scale - top - mid
    own_index = index[...]
    index_high = (own_index // 128).astype(f32)
    index_low = (own_index % 128).astype(f32)
    line = lax.broadcasted_iota(jnp.int32, (META, cols), 0)
    meta = jnp.zeros((META, cols), f32)
    for i, value in enumerate((top, mid, last, index_high, index_low)):
        meta = jnp.where(line == i, value, meta)
    ext[pl.ds(keep // 2, META), :] = meta.astype(bf16)

    acc_a[...] = jnp.zeros_like(acc_a)
    acc_b[...] = jnp.zeros_like(acc_b)
    acc_c[...] = jnp.zeros_like(acc_c)

    @pl.when(interior)
    def _():
        pl.semaphore_wait(barrier, 5)

    @pl.when(at_end)
    def _():
        pl.semaphore_wait(barrier, 4)

    def remote(src, dst, send, recv, peer):
        return pltpu.make_async_remote_copy(
            src_ref=src, dst_ref=dst, send_sem=send, recv_sem=recv, device_id=peer, device_id_type=MESH
        )

    def span(q):
        if isinstance(q, int) and q < 0:
            return pl.ds(0, head)
        return pl.ds(pl.multiple_of(head + q * piece, 16), piece)

    def number(half, q):
        return (2 * half + q % 2) * PIECES + q // 2

    def own_ref(q):
        if isinstance(q, int) and q < 0:
            return ext
        at = pl.multiple_of(number(g, q) * piece, piece)
        return w_all.at[pl.ds(at, piece), pl.ds(cols, cols)]

    def blast(q):
        return remote(own_ref(q), from_outer.at[span(q)], inner_send.at[q + 1], outer_recv.at[q + 1], {"wide": inner})

    def send_inner(q):
        return remote(
            to_inner.at[span(q)], from_inner.at[span(q)], inner_send.at[q + 1], inner_recv.at[q + 1], {"wide": inner}
        )

    def send_outer(q):
        return remote(
            to_outer.at[span(q)], from_inner.at[span(q)], outer_send.at[q + 1], inner_recv.at[q + 1], {"wide": outer}
        )

    def send_y(q):
        return remote(
            other.at[g, span(q)], other.at[g, span(q)], y_send.at[q + 1], y_recv.at[q + 1], {"groups": y}
        )

    def send_x(j):
        at = n * PIECES + j
        return remote(x_all.at[at], x_all.at[at], x_send.at[j], x_recv.at[j], {"narrow": n_x})

    def send_far(j):
        at = n_x * PIECES + j
        return remote(x_all.at[at], x_all.at[at], f_send.at[j], f_recv.at[j], {"narrow": n_core})

    own_slice = x_all.at[pl.ds(n * PIECES, PIECES)]
    send_core = remote(own_slice, own_slice, c_send, c_recv, {"narrow": n_core})

    def arrived(dst, sem):
        pltpu.make_async_copy(dst, dst, sem).wait()

    mine = place[w]
    inner_differs = mine != place[inner]
    outer_differs = mine != place[outer]
    total = 2 * PIECES

    @pl.when(at_end)
    def _():
        blast(-1).start()

    load_tok(0).wait()
    send_x(0).start()
    load_levels.wait()

    @pl.when(at_end)
    def _():
        def one(q, carry):
            blast(q).start()
            return carry
        lax.fori_loop(0, total, one, 0)

    for j in range(1, PIECES):
        load_tok(j).wait()
        send_x(j).start()
    send_core.start()
    load_base.wait()

    def near(q):
        @pl.when(interior)
        def _():
            arrived(from_outer.at[span(q)], outer_recv.at[q + 1])
            to_inner[span(q), :] = jnp.where(inner_differs, own_ref(q)[...], from_outer[span(q), :])
            send_inner(q).start()

    def far(q):
        arrived(from_inner.at[span(q)], inner_recv.at[q + 1])

        @pl.when(interior)
        def _():
            to_outer[span(q), :] = jnp.where(outer_differs, own_ref(q)[...], from_inner[span(q), :])
            send_outer(q).start()
            other[g, span(q), :] = jnp.where(outer_differs, from_outer[span(q), :], from_inner[span(q), :])

        @pl.when(at_end)
        def _():
            other[g, span(q), :] = from_inner[span(q), :]

        send_y(q).start()

    line_piece = lax.broadcasted_iota(jnp.int32, (piece, keep), 0)

    def picks(p, which):
        return (line_piece + p * piece == which).astype(f32).astype(bf16)

    def local(p):
        x = x_all[p]
        at = pl.multiple_of(p * piece, piece)
        acc_a[...] += jnp.dot(x, w_all[pl.ds(at, piece), :], preferred_element_type=f32)
        acc_c[...] += jnp.dot(x, picks(p, index[...]), preferred_element_type=f32)

    def foreign(half, q):
        p = number(half, q)
        both = jnp.concatenate([other[half, span(q), :], picks(p, other_index[...])], axis=1)
        acc_b[...] += jnp.dot(x_all[p], both, preferred_element_type=f32)

    def step(d):
        traced = not isinstance(d, int)
        if traced or d < PIECES:
            if not traced and d == 0:
                near(-1)
            near(2 * d)
            near(2 * d + 1)
        if traced or 1 <= d <= PIECES:
            if not traced and d == 1:
                far(-1)
                info = other[g, pl.ds(keep // 2, META), :].astype(f32)
                other_index[...] = (info[3:4] * 128.0 + info[4:5]).astype(jnp.int32)
            far(2 * d - 2)
            far(2 * d - 1)
        if traced or d < PIECES:
            arrived(x_all.at[n_x * PIECES + d], x_recv.at[d])
            send_far(d).start()
            local(n * PIECES + d)
            if not traced and d == 0:
                arrived(x_all.at[pl.ds(n_core * PIECES, PIECES)], c_recv)
            local(n_core * PIECES + d)
            local(n_x * PIECES + d)
        if traced or 1 <= d <= PIECES:
            arrived(x_all.at[n_far * PIECES + d - 1], f_recv.at[d - 1])
            local(n_far * PIECES + d - 1)
        if traced or d >= 2:
            for q in (2 * d - 4, 2 * d - 3):
                foreign(g, q)
            for q in (2 * d - 4, 2 * d - 3):
                arrived(other.at[y, span(q)], y_recv.at[q + 1])
                foreign(y, q)

    step(0)
    step(1)

    def middle(d, carry):
        step(d)
        return carry

    lax.fori_loop(2, PIECES, middle, 0)
    step(PIECES)
    step(PIECES + 1)
    arrived(other.at[y, span(-1)], y_recv.at[0])

    info = other[g, pl.ds(keep // 2, META), :].astype(f32)
    other_scale = info[0:1] + info[1:2] + info[2:3]
    other_values = jnp.concatenate(
        [other[0, pl.ds(0, keep // 2), :], other[1, pl.ds(0, keep // 2), :]], axis=0
    )
    own_update = acc_a[:, pl.ds(cols, cols)] * scale + jnp.dot(
        acc_c[...].astype(bf16), values[...], preferred_element_type=f32
    )
    other_update = acc_b[:, pl.ds(0, cols)] * other_scale + jnp.dot(
        acc_b[:, pl.ds(cols, keep)].astype(bf16), other_values, preferred_element_type=f32
    )
    square = (rows, rows)
    diagonal = lax.broadcasted_iota(jnp.int32, square, 0) == lax.broadcasted_iota(jnp.int32, square, 1)
    belongs = jnp.where(diagonal & (tenants[...] == mine), 1.0, 0.0)
    is_own = jnp.sum(belongs, axis=1, keepdims=True) > 0.5
    update = jnp.where(is_own, own_update, other_update).astype(bf16)
    out[...] = (acc_a[:, pl.ds(0, cols)] + update.astype(f32)).astype(bf16)

    def sent(copy):
        copy.wait_send()

    def ends(q, carry):
        sent(blast(q))
        return carry

    def middles(q, carry):
        sent(send_inner(q))
        sent(send_outer(q))
        return carry

    def alls(q, carry):
        sent(send_y(q))
        return carry

    def slices(j, carry):
        sent(send_x(j))
        sent(send_far(j))
        return carry

    @pl.when(at_end)
    def _():
        sent(blast(-1))
        lax.fori_loop(0, total, ends, 0)

    @pl.when(interior)
    def _():
        sent(send_inner(-1))
        sent(send_outer(-1))
        lax.fori_loop(0, total, middles, 0)

    sent(send_y(-1))
    lax.fori_loop(0, total, alls, 0)
    lax.fori_loop(0, PIECES, slices, 0)
    sent(send_core)


def delta_plan(
    tokens,
    tenant_ids,
    placement,
    base_weight,
    delta_levels,
    delta_scales,
    outlier_index,
    outlier_values,
):
    rows, width = tokens.shape
    depth, cols = base_weight.shape
    keep = outlier_index.shape[1]
    piece = width // PIECES
    slices = depth // width
    stream = keep // 2 + META + depth // 2
    parts = 2 * PIECES + 1
    bf16 = jnp.bfloat16
    vmem = pl.BlockSpec(memory_space=pltpu.VMEM)
    hbm = pl.BlockSpec(memory_space=pl.ANY)
    dma = pltpu.SemaphoreType.DMA
    return pl.pallas_call(
        kernel,
        out_shape=jax.ShapeDtypeStruct((rows, cols), bf16),
        in_specs=[pl.BlockSpec(memory_space=pltpu.SMEM), vmem, vmem, vmem, vmem, hbm, hbm, hbm],
        out_specs=vmem,
        scratch_shapes=[
            pltpu.VMEM((slices * PIECES, rows, piece), bf16),
            pltpu.VMEM((depth, 2 * cols), bf16),
            pltpu.VMEM((keep // 2 + META, cols), bf16),
            pltpu.VMEM((stream, cols), bf16),
            pltpu.VMEM((stream, cols), bf16),
            pltpu.VMEM((stream, cols), bf16),
            pltpu.VMEM((stream, cols), bf16),
            pltpu.VMEM((2, stream, cols), bf16),
            pltpu.VMEM((1, keep), jnp.int32),
            pltpu.VMEM((rows, 2 * cols), jnp.float32),
            pltpu.VMEM((rows, cols + keep), jnp.float32),
            pltpu.VMEM((rows, keep), jnp.float32),
            dma((2,)),
            dma((PIECES,)),
            dma((parts,)),
            dma((parts,)),
            dma((parts,)),
            dma((PIECES,)),
            dma((PIECES,)),
            dma,
            dma((parts,)),
            dma((parts,)),
            dma((parts,)),
            dma((PIECES,)),
            dma((PIECES,)),
            dma,
        ],
        compiler_params=pltpu.CompilerParams(
            collective_id=0, has_side_effects=True, vmem_limit_bytes=40 * 1024 * 1024
        ),
    )(
        placement,
        tenant_ids.reshape(1, rows),
        delta_scales,
        outlier_index,
        outlier_values[0],
        tokens,
        base_weight,
        delta_levels[0],
    )


def row_plan(
    tokens,
    tenant_ids,
    placement,
    base_weight,
    delta_levels,
    delta_scales,
    outlier_index,
    outlier_values,
):
    wide_count = lax.axis_size("wide")
    row_count = tenant_ids.shape[0]
    capacity = 5 * row_count // (2 * wide_count)
    positions = jnp.arange(row_count, dtype=jnp.int32)
    same_tenant = tenant_ids[:, None] == tenant_ids[None, :]
    earlier = positions[None, :] < positions[:, None]
    row_rank = jnp.sum((same_tenant & earlier).astype(jnp.int32), axis=1)
    devices = jnp.arange(wide_count, dtype=jnp.int32)
    holds_tenant = tenant_ids[:, None] == placement[None, :]
    holders = jnp.sum(holds_tenant.astype(jnp.int32), axis=1)
    same_peer = placement[:, None] == placement[None, :]
    before = devices[None, :] < devices[:, None]
    peer_rank = jnp.sum((same_peer & before).astype(jnp.int32), axis=1)
    replica = row_rank % holders
    target = holds_tenant & (peer_rank[None, :] == replica[:, None])
    holder_index = jnp.sum(jnp.where(target, devices[None, :], 0), axis=1)
    slot_index = holder_index * capacity + row_rank // holders
    source_row = (
        jnp.full((wide_count * capacity,), row_count, jnp.int32).at[slot_index].set(positions)
    )
    whole = lax.all_gather(tokens, "narrow", axis=1, tiled=True)
    base_part = jnp.dot(whole, base_weight, preferred_element_type=jnp.float32)
    levels = delta_levels[0]
    scales = delta_scales[0]
    picked_cols = outlier_index[0]
    outlier_rows = outlier_values[0]
    outgoing = jnp.take(whole, source_row, axis=0, mode="fill", fill_value=0).reshape(
        wide_count, capacity, whole.shape[1]
    )
    received = lax.all_to_all(outgoing, "wide", split_axis=0, concat_axis=0, tiled=True)
    product = (
        jnp.einsum("nid,df->nif", received, levels, preferred_element_type=jnp.float32) * scales
    )
    chosen = jnp.take(received, picked_cols, axis=2)
    product = product + jnp.einsum(
        "nik,kf->nif", chosen, outlier_rows, preferred_element_type=jnp.float32
    )
    returned_rows = lax.all_to_all(
        product.astype(jnp.bfloat16), "wide", split_axis=0, concat_axis=0, tiled=True
    )
    update = jnp.take(
        returned_rows.reshape(wide_count * capacity, returned_rows.shape[2]), slot_index, axis=0
    )
    return (base_part + update.astype(jnp.float32)).astype(jnp.bfloat16)


def solution(mesh):
    placed = (
        P(("groups", "wide"), "narrow"),
        P("wide"),
        P(),
        P(None, "narrow"),
        P("wide", None, "narrow"),
        P("wide", "narrow"),
        P("wide", None),
        P("wide", None, "narrow"),
    )
    few = mesh.shape["wide"] == 4 and mesh.shape["narrow"] == 4 and mesh.shape["groups"] == 2
    return jax.shard_map(
        delta_plan if few else row_plan,
        mesh=mesh,
        in_specs=placed,
        out_specs=P(("groups", "wide"), "narrow"),
        check_vma=False,
    )
```

```python
import functools

import jax
import jax.numpy as jnp
from jax import lax
from jax.experimental import pallas as pl
from jax.experimental.pallas import tpu as pltpu
from jax.sharding import PartitionSpec as P

MESH = pl.DeviceIdType.MESH
PIECES = 8
META = 16


def kernel(
    place, tenants, scales, index, values, tok, base, levels, out,
    x_all, w_all, ext, from_outer, from_inner, to_inner, to_outer, other, other_index,
    acc_a, acc_b, acc_c,
    load_sem, tok_sem,
    outer_recv, inner_recv, y_recv, x_recv, f_recv, c_recv,
    inner_send, outer_send, y_send, x_send, f_send, c_send,
):
    f32, bf16 = jnp.float32, jnp.bfloat16
    rows, cols = out.shape
    depth = base.shape[0]
    keep = values.shape[0]
    piece = x_all.shape[2]
    head = keep // 2 + META
    g = lax.axis_index("groups")
    w = lax.axis_index("wide")
    n = lax.axis_index("narrow")
    n_core = n + 1 - 2 * (n % 2)
    n_x = (n + 2) % 4
    n_far = n_x + 1 - 2 * (n_x % 2)
    low = w // 2 == 0
    at_end = (w == 0) | (w == 3)
    interior = (w == 1) | (w == 2)
    inner = jnp.where(low, w + 1, w - 1)
    outer = jnp.where(interior, jnp.where(low, w - 1, w + 1), w)
    y = 1 - g

    load_levels = pltpu.make_async_copy(levels, w_all.at[:, pl.ds(cols, cols)], load_sem.at[0])
    load_base = pltpu.make_async_copy(base, w_all.at[:, pl.ds(0, cols)], load_sem.at[1])

    def load_tok(j):
        return pltpu.make_async_copy(
            tok.at[:, pl.ds(j * piece, piece)], x_all.at[n * PIECES + j], tok_sem.at[j]
        )

    for j in range(PIECES):
        load_tok(j).start()
    load_levels.start()
    load_base.start()

    barrier = pltpu.get_barrier_semaphore()
    for peer in ({"narrow": n_core}, {"narrow": n_x}, {"groups": y}, {"wide": inner}):
        pl.semaphore_signal(barrier, inc=1, device_id=peer, device_id_type=MESH)

    @pl.when(interior)
    def _():
        pl.semaphore_signal(barrier, inc=1, device_id={"wide": outer}, device_id_type=MESH)

    ext[pl.ds(0, keep // 2), :] = values[pl.ds(pl.multiple_of(g * (keep // 2), keep // 2), keep // 2), :]
    scale = scales[...]
    top = scale.astype(bf16).astype(f32)
    mid = (scale - top).astype(bf16).astype(f32)
    last = scale - top - mid
    own_index = index[...]
    index_high = (own_index // 128).astype(f32)
    index_low = (own_index % 128).astype(f32)
    line = lax.broadcasted_iota(jnp.int32, (META, cols), 0)
    meta = jnp.zeros((META, cols), f32)
    for i, value in enumerate((top, mid, last, index_high, index_low)):
        meta = jnp.where(line == i, value, meta)
    ext[pl.ds(keep // 2, META), :] = meta.astype(bf16)

    acc_a[...] = jnp.zeros_like(acc_a)
    acc_b[...] = jnp.zeros_like(acc_b)
    acc_c[...] = jnp.zeros_like(acc_c)

    @pl.when(interior)
    def _():
        pl.semaphore_wait(barrier, 5)

    @pl.when(at_end)
    def _():
        pl.semaphore_wait(barrier, 4)

    def remote(src, dst, send, recv, peer):
        return pltpu.make_async_remote_copy(
            src_ref=src, dst_ref=dst, send_sem=send, recv_sem=recv, device_id=peer, device_id_type=MESH
        )

    def span(q):
        if isinstance(q, int) and q < 0:
            return pl.ds(0, head)
        return pl.ds(pl.multiple_of(head + q * piece, 16), piece)

    def number(half, q):
        return (2 * half + q % 2) * PIECES + q // 2

    def own_ref(q):
        if isinstance(q, int) and q < 0:
            return ext
        at = pl.multiple_of(number(g, q) * piece, piece)
        return w_all.at[pl.ds(at, piece), pl.ds(cols, cols)]

    def blast(q):
        return remote(own_ref(q), from_outer.at[span(q)], inner_send.at[q + 1], outer_recv.at[q + 1], {"wide": inner})

    def send_inner(q):
        return remote(
            to_inner.at[span(q)], from_inner.at[span(q)], inner_send.at[q + 1], inner_recv.at[q + 1], {"wide": inner}
        )

    def send_outer(q):
        return remote(
            to_outer.at[span(q)], from_inner.at[span(q)], outer_send.at[q + 1], inner_recv.at[q + 1], {"wide": outer}
        )

    def send_y(q):
        return remote(
            other.at[g, span(q)], other.at[g, span(q)], y_send.at[q + 1], y_recv.at[q + 1], {"groups": y}
        )

    def send_x(j):
        at = n * PIECES + j
        return remote(x_all.at[at], x_all.at[at], x_send.at[j], x_recv.at[j], {"narrow": n_x})

    def send_far(j):
        at = n_x * PIECES + j
        return remote(x_all.at[at], x_all.at[at], f_send.at[j], f_recv.at[j], {"narrow": n_core})

    own_slice = x_all.at[pl.ds(n * PIECES, PIECES)]
    send_core = remote(own_slice, own_slice, c_send, c_recv, {"narrow": n_core})

    def arrived(dst, sem):
        pltpu.make_async_copy(dst, dst, sem).wait()

    mine = place[w]
    inner_differs = mine != place[inner]
    outer_differs = mine != place[outer]
    total = 2 * PIECES

    @pl.when(at_end)
    def _():
        blast(-1).start()

    load_tok(0).wait()
    send_x(0).start()
    load_levels.wait()

    @pl.when(at_end)
    def _():
        def one(q, carry):
            blast(q).start()
            return carry
        lax.fori_loop(0, total, one, 0)

    for j in range(1, PIECES):
        load_tok(j).wait()
        send_x(j).start()
    send_core.start()
    load_base.wait()

    def near(q):
        @pl.when(interior)
        def _():
            arrived(from_outer.at[span(q)], outer_recv.at[q + 1])
            to_inner[span(q), :] = jnp.where(inner_differs, own_ref(q)[...], from_outer[span(q), :])
            send_inner(q).start()

    def far(q):
        arrived(from_inner.at[span(q)], inner_recv.at[q + 1])

        @pl.when(interior)
        def _():
            to_outer[span(q), :] = jnp.where(outer_differs, own_ref(q)[...], from_inner[span(q), :])
            send_outer(q).start()
            other[g, span(q), :] = jnp.where(outer_differs, from_outer[span(q), :], from_inner[span(q), :])

        @pl.when(at_end)
        def _():
            other[g, span(q), :] = from_inner[span(q), :]

        send_y(q).start()

    line_piece = lax.broadcasted_iota(jnp.int32, (piece, keep), 0)

    def picks(p, which):
        return (line_piece + p * piece == which).astype(f32).astype(bf16)

    def local(p):
        x = x_all[p]
        at = pl.multiple_of(p * piece, piece)
        acc_a[...] += jnp.dot(x, w_all[pl.ds(at, piece), :], preferred_element_type=f32)
        acc_c[...] += jnp.dot(x, picks(p, index[...]), preferred_element_type=f32)

    def foreign(half, q):
        p = number(half, q)
        both = jnp.concatenate([other[half, span(q), :], picks(p, other_index[...])], axis=1)
        acc_b[...] += jnp.dot(x_all[p], both, preferred_element_type=f32)

    def step(d):
        traced = not isinstance(d, int)
        if traced or d < PIECES:
            if not traced and d == 0:
                near(-1)
            near(2 * d)
            near(2 * d + 1)
        if traced or 1 <= d <= PIECES:
            if not traced and d == 1:
                far(-1)
                info = other[g, pl.ds(keep // 2, META), :].astype(f32)
                other_index[...] = (info[3:4] * 128.0 + info[4:5]).astype(jnp.int32)
            far(2 * d - 2)
            far(2 * d - 1)
        if traced or d < PIECES:
            arrived(x_all.at[n_x * PIECES + d], x_recv.at[d])
            send_far(d).start()
            local(n * PIECES + d)
            if not traced and d == 0:
                arrived(x_all.at[pl.ds(n_core * PIECES, PIECES)], c_recv)
            local(n_core * PIECES + d)
            local(n_x * PIECES + d)
        if traced or 1 <= d <= PIECES:
            arrived(x_all.at[n_far * PIECES + d - 1], f_recv.at[d - 1])
            local(n_far * PIECES + d - 1)
        if traced or d >= 2:
            for q in (2 * d - 4, 2 * d - 3):
                foreign(g, q)
            for q in (2 * d - 4, 2 * d - 3):
                arrived(other.at[y, span(q)], y_recv.at[q + 1])
                foreign(y, q)

    step(0)
    step(1)

    def middle(d, carry):
        step(d)
        return carry

    lax.fori_loop(2, PIECES, middle, 0)
    step(PIECES)
    step(PIECES + 1)
    arrived(other.at[y, span(-1)], y_recv.at[0])

    info = other[g, pl.ds(keep // 2, META), :].astype(f32)
    other_scale = info[0:1] + info[1:2] + info[2:3]
    other_values = jnp.concatenate(
        [other[0, pl.ds(0, keep // 2), :], other[1, pl.ds(0, keep // 2), :]], axis=0
    )
    own_update = acc_a[:, pl.ds(cols, cols)] * scale + jnp.dot(
        acc_c[...].astype(bf16), values[...], preferred_element_type=f32
    )
    other_update = acc_b[:, pl.ds(0, cols)] * other_scale + jnp.dot(
        acc_b[:, pl.ds(cols, keep)].astype(bf16), other_values, preferred_element_type=f32
    )
    square = (rows, rows)
    diagonal = lax.broadcasted_iota(jnp.int32, square, 0) == lax.broadcasted_iota(jnp.int32, square, 1)
    belongs = jnp.where(diagonal & (tenants[...] == mine), 1.0, 0.0)
    is_own = jnp.sum(belongs, axis=1, keepdims=True) > 0.5
    update = jnp.where(is_own, own_update, other_update).astype(bf16)
    out[...] = (acc_a[:, pl.ds(0, cols)] + update.astype(f32)).astype(bf16)

    def sent(copy):
        copy.wait_send()

    def ends(q, carry):
        sent(blast(q))
        return carry

    def middles(q, carry):
        sent(send_inner(q))
        sent(send_outer(q))
        return carry

    def alls(q, carry):
        sent(send_y(q))
        return carry

    def slices(j, carry):
        sent(send_x(j))
        sent(send_far(j))
        return carry

    @pl.when(at_end)
    def _():
        sent(blast(-1))
        lax.fori_loop(0, total, ends, 0)

    @pl.when(interior)
    def _():
        sent(send_inner(-1))
        sent(send_outer(-1))
        lax.fori_loop(0, total, middles, 0)

    sent(send_y(-1))
    lax.fori_loop(0, total, alls, 0)
    lax.fori_loop(0, PIECES, slices, 0)
    sent(send_core)


def delta_plan(
    tokens,
    tenant_ids,
    placement,
    base_weight,
    delta_levels,
    delta_scales,
    outlier_index,
    outlier_values,
):
    rows, width = tokens.shape
    depth, cols = base_weight.shape
    keep = outlier_index.shape[1]
    piece = width // PIECES
    slices = depth // width
    stream = keep // 2 + META + depth // 2
    parts = 2 * PIECES + 1
    bf16 = jnp.bfloat16
    vmem = pl.BlockSpec(memory_space=pltpu.VMEM)
    hbm = pl.BlockSpec(memory_space=pl.ANY)
    dma = pltpu.SemaphoreType.DMA
    return pl.pallas_call(
        kernel,
        out_shape=jax.ShapeDtypeStruct((rows, cols), bf16),
        in_specs=[pl.BlockSpec(memory_space=pltpu.SMEM), vmem, vmem, vmem, vmem, hbm, hbm, hbm],
        out_specs=vmem,
        scratch_shapes=[
            pltpu.VMEM((slices * PIECES, rows, piece), bf16),
            pltpu.VMEM((depth, 2 * cols), bf16),
            pltpu.VMEM((keep // 2 + META, cols), bf16),
            pltpu.VMEM((stream, cols), bf16),
            pltpu.VMEM((stream, cols), bf16),
            pltpu.VMEM((stream, cols), bf16),
            pltpu.VMEM((stream, cols), bf16),
            pltpu.VMEM((2, stream, cols), bf16),
            pltpu.VMEM((1, keep), jnp.int32),
            pltpu.VMEM((rows, 2 * cols), jnp.float32),
            pltpu.VMEM((rows, cols + keep), jnp.float32),
            pltpu.VMEM((rows, keep), jnp.float32),
            dma((2,)),
            dma((PIECES,)),
            dma((parts,)),
            dma((parts,)),
            dma((parts,)),
            dma((PIECES,)),
            dma((PIECES,)),
            dma,
            dma((parts,)),
            dma((parts,)),
            dma((parts,)),
            dma((PIECES,)),
            dma((PIECES,)),
            dma,
        ],
        compiler_params=pltpu.CompilerParams(
            collective_id=0, has_side_effects=True, vmem_limit_bytes=64 * 1024 * 1024 - 65536
        ),
    )(
        placement,
        tenant_ids.reshape(1, rows),
        delta_scales,
        outlier_index,
        outlier_values[0],
        tokens,
        base_weight,
        delta_levels[0],
    )


def row_plan(
    tokens,
    tenant_ids,
    placement,
    base_weight,
    delta_levels,
    delta_scales,
    outlier_index,
    outlier_values,
):
    wide_count = lax.axis_size("wide")
    row_count = tenant_ids.shape[0]
    capacity = 5 * row_count // (2 * wide_count)
    positions = jnp.arange(row_count, dtype=jnp.int32)
    same_tenant = tenant_ids[:, None] == tenant_ids[None, :]
    earlier = positions[None, :] < positions[:, None]
    row_rank = jnp.sum((same_tenant & earlier).astype(jnp.int32), axis=1)
    devices = jnp.arange(wide_count, dtype=jnp.int32)
    holds_tenant = tenant_ids[:, None] == placement[None, :]
    holders = jnp.sum(holds_tenant.astype(jnp.int32), axis=1)
    same_peer = placement[:, None] == placement[None, :]
    before = devices[None, :] < devices[:, None]
    peer_rank = jnp.sum((same_peer & before).astype(jnp.int32), axis=1)
    replica = row_rank % holders
    target = holds_tenant & (peer_rank[None, :] == replica[:, None])
    holder_index = jnp.sum(jnp.where(target, devices[None, :], 0), axis=1)
    slot_index = holder_index * capacity + row_rank // holders
    source_row = (
        jnp.full((wide_count * capacity,), row_count, jnp.int32).at[slot_index].set(positions)
    )
    whole = lax.all_gather(tokens, "narrow", axis=1, tiled=True)
    base_part = jnp.dot(whole, base_weight, preferred_element_type=jnp.float32)
    levels = delta_levels[0]
    scales = delta_scales[0]
    picked_cols = outlier_index[0]
    outlier_rows = outlier_values[0]
    outgoing = jnp.take(whole, source_row, axis=0, mode="fill", fill_value=0).reshape(
        wide_count, capacity, whole.shape[1]
    )
    received = lax.all_to_all(outgoing, "wide", split_axis=0, concat_axis=0, tiled=True)
    product = (
        jnp.einsum("nid,df->nif", received, levels, preferred_element_type=jnp.float32) * scales
    )
    chosen = jnp.take(received, picked_cols, axis=2)
    product = product + jnp.einsum(
        "nik,kf->nif", chosen, outlier_rows, preferred_element_type=jnp.float32
    )
    returned_rows = lax.all_to_all(
        product.astype(jnp.bfloat16), "wide", split_axis=0, concat_axis=0, tiled=True
    )
    update = jnp.take(
        returned_rows.reshape(wide_count * capacity, returned_rows.shape[2]), slot_index, axis=0
    )
    return (base_part + update.astype(jnp.float32)).astype(jnp.bfloat16)


def solution(mesh):
    placed = (
        P(("groups", "wide"), "narrow"),
        P("wide"),
        P(),
        P(None, "narrow"),
        P("wide", None, "narrow"),
        P("wide", "narrow"),
        P("wide", None),
        P("wide", None, "narrow"),
    )
    few = mesh.shape["wide"] == 4 and mesh.shape["narrow"] == 4 and mesh.shape["groups"] == 2
    return jax.shard_map(
        delta_plan if few else row_plan,
        mesh=mesh,
        in_specs=placed,
        out_specs=P(("groups", "wide"), "narrow"),
        check_vma=False,
    )
```

```python
import functools

import jax
import jax.numpy as jnp
from jax import lax
from jax.experimental import pallas as pl
from jax.experimental.pallas import tpu as pltpu
from jax.sharding import PartitionSpec as P

MESH = pl.DeviceIdType.MESH
PIECES = 8
META = 16


def lookup(w, table):
    value = jnp.int32(table[0])
    for i in range(1, len(table)):
        value = jnp.where(w == i, jnp.int32(table[i]), value)
    return value


def routes(same):
    held = [0]
    for equal in same:
        held.append(held[-1] if equal else 1 - held[-1])
    count = len(held)
    parent = []
    for w in range(count):
        far = [(abs(v - w), v) for v in range(count) if held[v] != held[w]]
        parent.append(w + 1 if min(far)[1] > w else w - 1)
    own, passed = {}, {}
    for name, shift in (("low", -1), ("high", 1)):
        child = [0 <= w + shift < count and parent[w + shift] == w for w in range(count)]
        own[name] = [int(child[w] and held[w + shift] != held[w]) for w in range(count)]
        passed[name] = [int(child[w] and held[w + shift] == held[w]) for w in range(count)]
    return own, passed


def kernel(
    same, place, tenants, scales, index, values, tok, base, levels, out,
    x_all, w_all, ext, other, other_index,
    acc_a, acc_b, acc_c,
    load_sem, tok_sem,
    z_recv, y_recv, x_recv, f_recv, c_recv,
    low_send, high_send, y_send, x_send, f_send, c_send,
):
    f32, bf16 = jnp.float32, jnp.bfloat16
    rows, cols = out.shape
    depth = base.shape[0]
    keep = values.shape[0]
    piece = x_all.shape[2]
    head = keep // 2 + META
    g = lax.axis_index("groups")
    w = lax.axis_index("wide")
    n = lax.axis_index("narrow")
    n_core = n + 1 - 2 * (n % 2)
    n_x = (n + 2) % 4
    n_far = n_x + 1 - 2 * (n_x % 2)
    low = w // 2 == 0
    at_end = (w == 0) | (w == 3)
    interior = (w == 1) | (w == 2)
    inner = jnp.where(low, w + 1, w - 1)
    outer = jnp.where(interior, jnp.where(low, w - 1, w + 1), w)
    y = 1 - g

    load_levels = pltpu.make_async_copy(levels, w_all.at[:, pl.ds(cols, cols)], load_sem.at[0])
    load_base = pltpu.make_async_copy(base, w_all.at[:, pl.ds(0, cols)], load_sem.at[1])

    def load_tok(j):
        return pltpu.make_async_copy(
            tok.at[:, pl.ds(j * piece, piece)], x_all.at[n * PIECES + j], tok_sem.at[j]
        )

    for j in range(PIECES):
        load_tok(j).start()
    load_levels.start()
    load_base.start()

    barrier = pltpu.get_barrier_semaphore()
    for peer in ({"narrow": n_core}, {"narrow": n_x}, {"groups": y}, {"wide": inner}):
        pl.semaphore_signal(barrier, inc=1, device_id=peer, device_id_type=MESH)

    @pl.when(interior)
    def _():
        pl.semaphore_signal(barrier, inc=1, device_id={"wide": outer}, device_id_type=MESH)

    ext[pl.ds(0, keep // 2), :] = values[pl.ds(pl.multiple_of(g * (keep // 2), keep // 2), keep // 2), :]
    scale = scales[...]
    top = scale.astype(bf16).astype(f32)
    mid = (scale - top).astype(bf16).astype(f32)
    last = scale - top - mid
    own_index = index[...]
    index_high = (own_index // 128).astype(f32)
    index_low = (own_index % 128).astype(f32)
    line = lax.broadcasted_iota(jnp.int32, (META, cols), 0)
    meta = jnp.zeros((META, cols), f32)
    for i, value in enumerate((top, mid, last, index_high, index_low)):
        meta = jnp.where(line == i, value, meta)
    ext[pl.ds(keep // 2, META), :] = meta.astype(bf16)

    acc_a[...] = jnp.zeros_like(acc_a)
    acc_b[...] = jnp.zeros_like(acc_b)
    acc_c[...] = jnp.zeros_like(acc_c)

    @pl.when(interior)
    def _():
        pl.semaphore_wait(barrier, 5)

    @pl.when(at_end)
    def _():
        pl.semaphore_wait(barrier, 4)

    def remote(src, dst, send, recv, peer):
        return pltpu.make_async_remote_copy(
            src_ref=src, dst_ref=dst, send_sem=send, recv_sem=recv, device_id=peer, device_id_type=MESH
        )

    def span(q):
        if isinstance(q, int) and q < 0:
            return pl.ds(0, head)
        return pl.ds(pl.multiple_of(head + q * piece, 16), piece)

    def number(half, q):
        return (2 * half + q % 2) * PIECES + q // 2

    def own_ref(q):
        if isinstance(q, int) and q < 0:
            return ext
        at = pl.multiple_of(number(g, q) * piece, piece)
        return w_all.at[pl.ds(at, piece), pl.ds(cols, cols)]

    own_to, pass_to = routes(same)
    sides = (("low", jnp.maximum(w - 1, 0), low_send), ("high", jnp.minimum(w + 1, 3), high_send))

    def give(side, q):
        name, peer, sems = side
        return remote(own_ref(q), other.at[g, span(q)], sems.at[q + 1], z_recv.at[q + 1], {"wide": peer})

    def hand_on(side, q):
        name, peer, sems = side
        at = other.at[g, span(q)]
        return remote(at, at, sems.at[q + 1], z_recv.at[q + 1], {"wide": peer})

    def send_y(q):
        return remote(
            other.at[g, span(q)], other.at[g, span(q)], y_send.at[q + 1], y_recv.at[q + 1], {"groups": y}
        )

    def send_x(j):
        at = n * PIECES + j
        return remote(x_all.at[at], x_all.at[at], x_send.at[j], x_recv.at[j], {"narrow": n_x})

    def send_far(j):
        at = n_x * PIECES + j
        return remote(x_all.at[at], x_all.at[at], f_send.at[j], f_recv.at[j], {"narrow": n_core})

    own_slice = x_all.at[pl.ds(n * PIECES, PIECES)]
    send_core = remote(own_slice, own_slice, c_send, c_recv, {"narrow": n_core})

    def arrived(dst, sem):
        pltpu.make_async_copy(dst, dst, sem).wait()

    mine = place[w]
    total = 2 * PIECES

    for side in sides:
        if any(own_to[side[0]]):
            @pl.when(lookup(w, own_to[side[0]]) == 1)
            def _(side=side):
                give(side, -1).start()

    load_tok(0).wait()
    send_x(0).start()
    load_levels.wait()

    for side in sides:
        if any(own_to[side[0]]):
            @pl.when(lookup(w, own_to[side[0]]) == 1)
            def _(side=side):
                def one(q, carry):
                    give(side, q).start()
                    return carry
                lax.fori_loop(0, total, one, 0)

    for j in range(1, PIECES):
        load_tok(j).wait()
        send_x(j).start()
    send_core.start()
    load_base.wait()

    def take(q):
        arrived(other.at[g, span(q)], z_recv.at[q + 1])
        for side in sides:
            if any(pass_to[side[0]]):
                @pl.when(lookup(w, pass_to[side[0]]) == 1)
                def _(side=side):
                    hand_on(side, q).start()
        send_y(q).start()

    line_piece = lax.broadcasted_iota(jnp.int32, (piece, keep), 0)

    def picks(p, which):
        return (line_piece + p * piece == which).astype(f32).astype(bf16)

    def local(p):
        x = x_all[p]
        at = pl.multiple_of(p * piece, piece)
        acc_a[...] += jnp.dot(x, w_all[pl.ds(at, piece), :], preferred_element_type=f32)
        acc_c[...] += jnp.dot(x, picks(p, index[...]), preferred_element_type=f32)

    def foreign(half, q):
        p = number(half, q)
        both = jnp.concatenate([other[half, span(q), :], picks(p, other_index[...])], axis=1)
        acc_b[...] += jnp.dot(x_all[p], both, preferred_element_type=f32)

    def step(d):
        traced = not isinstance(d, int)
        if traced or d < PIECES:
            arrived(x_all.at[n_x * PIECES + d], x_recv.at[d])
            send_far(d).start()
            if not traced and d == 0:
                local(n * PIECES)
                arrived(x_all.at[pl.ds(n_core * PIECES, PIECES)], c_recv)
                take(-1)
                info = other[g, pl.ds(keep // 2, META), :].astype(f32)
                other_index[...] = (info[3:4] * 128.0 + info[4:5]).astype(jnp.int32)
            take(2 * d)
            if traced or d > 0:
                local(n * PIECES + d)
            local(n_core * PIECES + d)
            take(2 * d + 1)
            local(n_x * PIECES + d)
        if traced or 1 <= d <= PIECES:
            arrived(x_all.at[n_far * PIECES + d - 1], f_recv.at[d - 1])
            local(n_far * PIECES + d - 1)
            for q in (2 * d - 2, 2 * d - 1):
                foreign(g, q)
        if traced or d >= 2:
            for q in (2 * d - 4, 2 * d - 3):
                arrived(other.at[y, span(q)], y_recv.at[q + 1])
                foreign(y, q)

    step(0)
    step(1)

    def middle(d, carry):
        step(d)
        return carry

    lax.fori_loop(2, PIECES, middle, 0)
    step(PIECES)
    step(PIECES + 1)
    arrived(other.at[y, span(-1)], y_recv.at[0])

    info = other[g, pl.ds(keep // 2, META), :].astype(f32)
    other_scale = info[0:1] + info[1:2] + info[2:3]
    other_values = jnp.concatenate(
        [other[0, pl.ds(0, keep // 2), :], other[1, pl.ds(0, keep // 2), :]], axis=0
    )
    own_update = acc_a[:, pl.ds(cols, cols)] * scale + jnp.dot(
        acc_c[...].astype(bf16), values[...], preferred_element_type=f32
    )
    other_update = acc_b[:, pl.ds(0, cols)] * other_scale + jnp.dot(
        acc_b[:, pl.ds(cols, keep)].astype(bf16), other_values, preferred_element_type=f32
    )
    square = (rows, rows)
    diagonal = lax.broadcasted_iota(jnp.int32, square, 0) == lax.broadcasted_iota(jnp.int32, square, 1)
    belongs = jnp.where(diagonal & (tenants[...] == mine), 1.0, 0.0)
    is_own = jnp.sum(belongs, axis=1, keepdims=True) > 0.5
    update = jnp.where(is_own, own_update, other_update).astype(bf16)
    out[...] = (acc_a[:, pl.ds(0, cols)] + update.astype(f32)).astype(bf16)

    def sent(copy):
        copy.wait_send()

    def alls(q, carry):
        sent(send_y(q))
        return carry

    def slices(j, carry):
        sent(send_x(j))
        sent(send_far(j))
        return carry

    for side in sides:
        for table, copy in ((own_to, give), (pass_to, hand_on)):
            if any(table[side[0]]):
                @pl.when(lookup(w, table[side[0]]) == 1)
                def _(side=side, copy=copy):
                    sent(copy(side, -1))

                    def one(q, carry):
                        sent(copy(side, q))
                        return carry
                    lax.fori_loop(0, total, one, 0)

    sent(send_y(-1))
    lax.fori_loop(0, total, alls, 0)
    lax.fori_loop(0, PIECES, slices, 0)
    sent(send_core)


def delta_plan(
    tokens,
    tenant_ids,
    placement,
    base_weight,
    delta_levels,
    delta_scales,
    outlier_index,
    outlier_values,
):
    rows, width = tokens.shape
    depth, cols = base_weight.shape
    keep = outlier_index.shape[1]
    piece = width // PIECES
    slices = depth // width
    stream = keep // 2 + META + depth // 2
    parts = 2 * PIECES + 1
    bf16 = jnp.bfloat16
    vmem = pl.BlockSpec(memory_space=pltpu.VMEM)
    hbm = pl.BlockSpec(memory_space=pl.ANY)
    dma = pltpu.SemaphoreType.DMA
    call = lambda same, ident: pl.pallas_call(
        functools.partial(kernel, same),
        out_shape=jax.ShapeDtypeStruct((rows, cols), bf16),
        in_specs=[pl.BlockSpec(memory_space=pltpu.SMEM), vmem, vmem, vmem, vmem, hbm, hbm, hbm],
        out_specs=vmem,
        scratch_shapes=[
            pltpu.VMEM((slices * PIECES, rows, piece), bf16),
            pltpu.VMEM((depth, 2 * cols), bf16),
            pltpu.VMEM((keep // 2 + META, cols), bf16),
            pltpu.VMEM((2, stream, cols), bf16),
            pltpu.VMEM((1, keep), jnp.int32),
            pltpu.VMEM((rows, 2 * cols), jnp.float32),
            pltpu.VMEM((rows, cols + keep), jnp.float32),
            pltpu.VMEM((rows, keep), jnp.float32),
            dma((2,)),
            dma((PIECES,)),
            dma((parts,)),
            dma((parts,)),
            dma((PIECES,)),
            dma((PIECES,)),
            dma,
            dma((parts,)),
            dma((parts,)),
            dma((parts,)),
            dma((PIECES,)),
            dma((PIECES,)),
            dma,
        ],
        compiler_params=pltpu.CompilerParams(
            collective_id=ident, has_side_effects=True, vmem_limit_bytes=64 * 1024 * 1024 - 65536
        ),
    )

    ways = [(a, b, c) for a in (False, True) for b in (False, True) for c in (False, True)][:-1]
    equal = (placement[:-1] == placement[1:]).astype(jnp.int32)
    which = jnp.minimum(equal[0] * 4 + equal[1] * 2 + equal[2], len(ways) - 1)
    return lax.switch(
        which,
        [call(same, ident) for ident, same in enumerate(ways)],
        placement,
        tenant_ids.reshape(1, rows),
        delta_scales,
        outlier_index,
        outlier_values[0],
        tokens,
        base_weight,
        delta_levels[0],
    )


def row_plan(
    tokens,
    tenant_ids,
    placement,
    base_weight,
    delta_levels,
    delta_scales,
    outlier_index,
    outlier_values,
):
    wide_count = lax.axis_size("wide")
    row_count = tenant_ids.shape[0]
    capacity = 5 * row_count // (2 * wide_count)
    positions = jnp.arange(row_count, dtype=jnp.int32)
    same_tenant = tenant_ids[:, None] == tenant_ids[None, :]
    earlier = positions[None, :] < positions[:, None]
    row_rank = jnp.sum((same_tenant & earlier).astype(jnp.int32), axis=1)
    devices = jnp.arange(wide_count, dtype=jnp.int32)
    holds_tenant = tenant_ids[:, None] == placement[None, :]
    holders = jnp.sum(holds_tenant.astype(jnp.int32), axis=1)
    same_peer = placement[:, None] == placement[None, :]
    before = devices[None, :] < devices[:, None]
    peer_rank = jnp.sum((same_peer & before).astype(jnp.int32), axis=1)
    replica = row_rank % holders
    target = holds_tenant & (peer_rank[None, :] == replica[:, None])
    holder_index = jnp.sum(jnp.where(target, devices[None, :], 0), axis=1)
    slot_index = holder_index * capacity + row_rank // holders
    source_row = (
        jnp.full((wide_count * capacity,), row_count, jnp.int32).at[slot_index].set(positions)
    )
    whole = lax.all_gather(tokens, "narrow", axis=1, tiled=True)
    base_part = jnp.dot(whole, base_weight, preferred_element_type=jnp.float32)
    levels = delta_levels[0]
    scales = delta_scales[0]
    picked_cols = outlier_index[0]
    outlier_rows = outlier_values[0]
    outgoing = jnp.take(whole, source_row, axis=0, mode="fill", fill_value=0).reshape(
        wide_count, capacity, whole.shape[1]
    )
    received = lax.all_to_all(outgoing, "wide", split_axis=0, concat_axis=0, tiled=True)
    product = (
        jnp.einsum("nid,df->nif", received, levels, preferred_element_type=jnp.float32) * scales
    )
    chosen = jnp.take(received, picked_cols, axis=2)
    product = product + jnp.einsum(
        "nik,kf->nif", chosen, outlier_rows, preferred_element_type=jnp.float32
    )
    returned_rows = lax.all_to_all(
        product.astype(jnp.bfloat16), "wide", split_axis=0, concat_axis=0, tiled=True
    )
    update = jnp.take(
        returned_rows.reshape(wide_count * capacity, returned_rows.shape[2]), slot_index, axis=0
    )
    return (base_part + update.astype(jnp.float32)).astype(jnp.bfloat16)


def solution(mesh):
    placed = (
        P(("groups", "wide"), "narrow"),
        P("wide"),
        P(),
        P(None, "narrow"),
        P("wide", None, "narrow"),
        P("wide", "narrow"),
        P("wide", None),
        P("wide", None, "narrow"),
    )
    few = mesh.shape["wide"] == 4 and mesh.shape["narrow"] == 4 and mesh.shape["groups"] == 2
    return jax.shard_map(
        delta_plan if few else row_plan,
        mesh=mesh,
        in_specs=placed,
        out_specs=P(("groups", "wide"), "narrow"),
        check_vma=False,
    )
```

```python
import functools

import jax
import jax.numpy as jnp
from jax import lax
from jax.experimental import pallas as pl
from jax.experimental.pallas import tpu as pltpu
from jax.sharding import PartitionSpec as P

MESH = pl.DeviceIdType.MESH
PIECES = 8
META = 16


def lookup(w, table):
    value = jnp.int32(table[0])
    for i in range(1, len(table)):
        value = jnp.where(w == i, jnp.int32(table[i]), value)
    return value


def routes(same):
    held = [0]
    for equal in same:
        held.append(held[-1] if equal else 1 - held[-1])
    count = len(held)
    parent = []
    for w in range(count):
        far = [(abs(v - w), v) for v in range(count) if held[v] != held[w]]
        parent.append(w + 1 if min(far)[1] > w else w - 1)
    own, passed = {}, {}
    for name, shift in (("low", -1), ("high", 1)):
        child = [0 <= w + shift < count and parent[w + shift] == w for w in range(count)]
        own[name] = [int(child[w] and held[w + shift] != held[w]) for w in range(count)]
        passed[name] = [int(child[w] and held[w + shift] == held[w]) for w in range(count)]
    return own, passed


def kernel(
    same, place, tenants, scales, index, values, tok, base, levels, out,
    x_all, w_all, ext, other, other_index,
    acc_a, acc_b, acc_c,
    load_sem, tok_sem,
    z_recv, y_recv, x_recv, f_recv, c_recv,
    low_send, high_send, y_send, x_send, f_send, c_send,
):
    f32, bf16 = jnp.float32, jnp.bfloat16
    rows, cols = out.shape
    depth = base.shape[0]
    keep = values.shape[0]
    piece = x_all.shape[2]
    head = keep // 2 + META
    g = lax.axis_index("groups")
    w = lax.axis_index("wide")
    n = lax.axis_index("narrow")
    n_core = n + 1 - 2 * (n % 2)
    n_x = (n + 2) % 4
    n_far = n_x + 1 - 2 * (n_x % 2)
    low = w // 2 == 0
    at_end = (w == 0) | (w == 3)
    interior = (w == 1) | (w == 2)
    inner = jnp.where(low, w + 1, w - 1)
    outer = jnp.where(interior, jnp.where(low, w - 1, w + 1), w)
    y = 1 - g

    load_levels = pltpu.make_async_copy(levels, w_all.at[:, pl.ds(cols, cols)], load_sem.at[0])
    load_base = pltpu.make_async_copy(base, w_all.at[:, pl.ds(0, cols)], load_sem.at[1])

    def load_tok(j):
        return pltpu.make_async_copy(
            tok.at[:, pl.ds(j * piece, piece)], x_all.at[n * PIECES + j], tok_sem.at[j]
        )

    for j in range(PIECES):
        load_tok(j).start()
    load_levels.start()
    load_base.start()

    barrier = pltpu.get_barrier_semaphore()
    for peer in ({"narrow": n_core}, {"narrow": n_x}, {"groups": y}, {"wide": inner}):
        pl.semaphore_signal(barrier, inc=1, device_id=peer, device_id_type=MESH)

    @pl.when(interior)
    def _():
        pl.semaphore_signal(barrier, inc=1, device_id={"wide": outer}, device_id_type=MESH)

    ext[pl.ds(0, keep // 2), :] = values[pl.ds(pl.multiple_of(g * (keep // 2), keep // 2), keep // 2), :]
    scale = scales[...]
    top = scale.astype(bf16).astype(f32)
    mid = (scale - top).astype(bf16).astype(f32)
    last = scale - top - mid
    own_index = index[...]
    index_high = (own_index // 128).astype(f32)
    index_low = (own_index % 128).astype(f32)
    line = lax.broadcasted_iota(jnp.int32, (META, cols), 0)
    meta = jnp.zeros((META, cols), f32)
    for i, value in enumerate((top, mid, last, index_high, index_low)):
        meta = jnp.where(line == i, value, meta)
    ext[pl.ds(keep // 2, META), :] = meta.astype(bf16)

    acc_a[...] = jnp.zeros_like(acc_a)
    acc_b[...] = jnp.zeros_like(acc_b)
    acc_c[...] = jnp.zeros_like(acc_c)

    @pl.when(interior)
    def _():
        pl.semaphore_wait(barrier, 5)

    @pl.when(at_end)
    def _():
        pl.semaphore_wait(barrier, 4)

    def remote(src, dst, send, recv, peer):
        return pltpu.make_async_remote_copy(
            src_ref=src, dst_ref=dst, send_sem=send, recv_sem=recv, device_id=peer, device_id_type=MESH
        )

    def span(q):
        if isinstance(q, int) and q < 0:
            return pl.ds(0, head)
        return pl.ds(pl.multiple_of(head + q * piece, 16), piece)

    def number(half, q):
        return (2 * half + q % 2) * PIECES + q // 2

    def own_ref(q):
        if isinstance(q, int) and q < 0:
            return ext
        at = pl.multiple_of(number(g, q) * piece, piece)
        return w_all.at[pl.ds(at, piece), pl.ds(cols, cols)]

    own_to, pass_to = routes(same)
    sides = (("low", jnp.maximum(w - 1, 0), low_send), ("high", jnp.minimum(w + 1, 3), high_send))

    def give(side, q):
        name, peer, sems = side
        return remote(own_ref(q), other.at[g, span(q)], sems.at[q + 1], z_recv.at[q + 1], {"wide": peer})

    def hand_on(side, q):
        name, peer, sems = side
        at = other.at[g, span(q)]
        return remote(at, at, sems.at[q + 1], z_recv.at[q + 1], {"wide": peer})

    def send_y(q):
        return remote(
            other.at[g, span(q)], other.at[g, span(q)], y_send.at[q + 1], y_recv.at[q + 1], {"groups": y}
        )

    def send_x(j):
        at = n * PIECES + j
        return remote(x_all.at[at], x_all.at[at], x_send.at[j], x_recv.at[j], {"narrow": n_x})

    def send_far(j):
        at = n_x * PIECES + j
        return remote(x_all.at[at], x_all.at[at], f_send.at[j], f_recv.at[j], {"narrow": n_core})

    own_slice = x_all.at[pl.ds(n * PIECES, PIECES)]
    send_core = remote(own_slice, own_slice, c_send, c_recv, {"narrow": n_core})

    def arrived(dst, sem):
        pltpu.make_async_copy(dst, dst, sem).wait()

    mine = place[w]
    total = 2 * PIECES

    for side in sides:
        if any(own_to[side[0]]):
            @pl.when(lookup(w, own_to[side[0]]) == 1)
            def _(side=side):
                give(side, -1).start()

    load_tok(0).wait()
    send_x(0).start()
    load_levels.wait()

    for side in sides:
        if any(own_to[side[0]]):
            @pl.when(lookup(w, own_to[side[0]]) == 1)
            def _(side=side):
                def one(q, carry):
                    give(side, q).start()
                    return carry
                lax.fori_loop(0, total, one, 0)

    for j in range(1, PIECES):
        load_tok(j).wait()
        send_x(j).start()
    send_core.start()
    load_base.wait()

    def take(q):
        arrived(other.at[g, span(q)], z_recv.at[q + 1])
        for side in sides:
            if any(pass_to[side[0]]):
                @pl.when(lookup(w, pass_to[side[0]]) == 1)
                def _(side=side):
                    hand_on(side, q).start()
        send_y(q).start()

    line_piece = lax.broadcasted_iota(jnp.int32, (piece, keep), 0)

    def picks(p, which):
        return (line_piece + p * piece == which).astype(f32).astype(bf16)

    def local(p):
        x = x_all[p]
        at = pl.multiple_of(p * piece, piece)
        acc_a[...] += jnp.dot(x, w_all[pl.ds(at, piece), :], preferred_element_type=f32)
        acc_c[...] += jnp.dot(x, picks(p, index[...]), preferred_element_type=f32)

    def foreign(half, q):
        p = number(half, q)
        both = jnp.concatenate([other[half, span(q), :], picks(p, other_index[...])], axis=1)
        acc_b[...] += jnp.dot(x_all[p], both, preferred_element_type=f32)

    def step(d):
        traced = not isinstance(d, int)
        if traced or d < PIECES:
            if not traced and d == 0:
                take(-1)
            take(2 * d)
            take(2 * d + 1)
            arrived(x_all.at[n_x * PIECES + d], x_recv.at[d])
            send_far(d).start()
            if not traced and d == 0:
                info = other[g, pl.ds(keep // 2, META), :].astype(f32)
                other_index[...] = (info[3:4] * 128.0 + info[4:5]).astype(jnp.int32)
                arrived(x_all.at[pl.ds(n_core * PIECES, PIECES)], c_recv)
            local(n * PIECES + d)
            local(n_core * PIECES + d)
            local(n_x * PIECES + d)
        if traced or 1 <= d <= PIECES:
            arrived(x_all.at[n_far * PIECES + d - 1], f_recv.at[d - 1])
            local(n_far * PIECES + d - 1)
            for q in (2 * d - 2, 2 * d - 1):
                foreign(g, q)
        if traced or d >= 2:
            for q in (2 * d - 4, 2 * d - 3):
                arrived(other.at[y, span(q)], y_recv.at[q + 1])
                foreign(y, q)

    step(0)
    step(1)

    def middle(d, carry):
        step(d)
        return carry

    lax.fori_loop(2, PIECES, middle, 0)
    step(PIECES)
    step(PIECES + 1)
    arrived(other.at[y, span(-1)], y_recv.at[0])

    info = other[g, pl.ds(keep // 2, META), :].astype(f32)
    other_scale = info[0:1] + info[1:2] + info[2:3]
    other_values = jnp.concatenate(
        [other[0, pl.ds(0, keep // 2), :], other[1, pl.ds(0, keep // 2), :]], axis=0
    )
    own_update = acc_a[:, pl.ds(cols, cols)] * scale + jnp.dot(
        acc_c[...].astype(bf16), values[...], preferred_element_type=f32
    )
    other_update = acc_b[:, pl.ds(0, cols)] * other_scale + jnp.dot(
        acc_b[:, pl.ds(cols, keep)].astype(bf16), other_values, preferred_element_type=f32
    )
    square = (rows, rows)
    diagonal = lax.broadcasted_iota(jnp.int32, square, 0) == lax.broadcasted_iota(jnp.int32, square, 1)
    belongs = jnp.where(diagonal & (tenants[...] == mine), 1.0, 0.0)
    is_own = jnp.sum(belongs, axis=1, keepdims=True) > 0.5
    update = jnp.where(is_own, own_update, other_update).astype(bf16)
    out[...] = (acc_a[:, pl.ds(0, cols)] + update.astype(f32)).astype(bf16)

    def sent(copy):
        copy.wait_send()

    def alls(q, carry):
        sent(send_y(q))
        return carry

    def slices(j, carry):
        sent(send_x(j))
        sent(send_far(j))
        return carry

    for side in sides:
        for table, copy in ((own_to, give), (pass_to, hand_on)):
            if any(table[side[0]]):
                @pl.when(lookup(w, table[side[0]]) == 1)
                def _(side=side, copy=copy):
                    sent(copy(side, -1))

                    def one(q, carry):
                        sent(copy(side, q))
                        return carry
                    lax.fori_loop(0, total, one, 0)

    sent(send_y(-1))
    lax.fori_loop(0, total, alls, 0)
    lax.fori_loop(0, PIECES, slices, 0)
    sent(send_core)


def delta_plan(
    tokens,
    tenant_ids,
    placement,
    base_weight,
    delta_levels,
    delta_scales,
    outlier_index,
    outlier_values,
):
    rows, width = tokens.shape
    depth, cols = base_weight.shape
    keep = outlier_index.shape[1]
    piece = width // PIECES
    slices = depth // width
    stream = keep // 2 + META + depth // 2
    parts = 2 * PIECES + 1
    bf16 = jnp.bfloat16
    vmem = pl.BlockSpec(memory_space=pltpu.VMEM)
    hbm = pl.BlockSpec(memory_space=pl.ANY)
    dma = pltpu.SemaphoreType.DMA
    call = lambda same, ident: pl.pallas_call(
        functools.partial(kernel, same),
        out_shape=jax.ShapeDtypeStruct((rows, cols), bf16),
        in_specs=[pl.BlockSpec(memory_space=pltpu.SMEM), vmem, vmem, vmem, vmem, hbm, hbm, hbm],
        out_specs=vmem,
        scratch_shapes=[
            pltpu.VMEM((slices * PIECES, rows, piece), bf16),
            pltpu.VMEM((depth, 2 * cols), bf16),
            pltpu.VMEM((keep // 2 + META, cols), bf16),
            pltpu.VMEM((2, stream, cols), bf16),
            pltpu.VMEM((1, keep), jnp.int32),
            pltpu.VMEM((rows, 2 * cols), jnp.float32),
            pltpu.VMEM((rows, cols + keep), jnp.float32),
            pltpu.VMEM((rows, keep), jnp.float32),
            dma((2,)),
            dma((PIECES,)),
            dma((parts,)),
            dma((parts,)),
            dma((PIECES,)),
            dma((PIECES,)),
            dma,
            dma((parts,)),
            dma((parts,)),
            dma((parts,)),
            dma((PIECES,)),
            dma((PIECES,)),
            dma,
        ],
        compiler_params=pltpu.CompilerParams(
            collective_id=ident, has_side_effects=True, vmem_limit_bytes=64 * 1024 * 1024 - 65536
        ),
    )

    ways = [(a, b, c) for a in (False, True) for b in (False, True) for c in (False, True)][:-1]
    equal = (placement[:-1] == placement[1:]).astype(jnp.int32)
    which = jnp.minimum(equal[0] * 4 + equal[1] * 2 + equal[2], len(ways) - 1)
    return lax.switch(
        which,
        [call(same, ident) for ident, same in enumerate(ways)],
        placement,
        tenant_ids.reshape(1, rows),
        delta_scales,
        outlier_index,
        outlier_values[0],
        tokens,
        base_weight,
        delta_levels[0],
    )


def row_plan(
    tokens,
    tenant_ids,
    placement,
    base_weight,
    delta_levels,
    delta_scales,
    outlier_index,
    outlier_values,
):
    wide_count = lax.axis_size("wide")
    row_count = tenant_ids.shape[0]
    capacity = 5 * row_count // (2 * wide_count)
    positions = jnp.arange(row_count, dtype=jnp.int32)
    same_tenant = tenant_ids[:, None] == tenant_ids[None, :]
    earlier = positions[None, :] < positions[:, None]
    row_rank = jnp.sum((same_tenant & earlier).astype(jnp.int32), axis=1)
    devices = jnp.arange(wide_count, dtype=jnp.int32)
    holds_tenant = tenant_ids[:, None] == placement[None, :]
    holders = jnp.sum(holds_tenant.astype(jnp.int32), axis=1)
    same_peer = placement[:, None] == placement[None, :]
    before = devices[None, :] < devices[:, None]
    peer_rank = jnp.sum((same_peer & before).astype(jnp.int32), axis=1)
    replica = row_rank % holders
    target = holds_tenant & (peer_rank[None, :] == replica[:, None])
    holder_index = jnp.sum(jnp.where(target, devices[None, :], 0), axis=1)
    slot_index = holder_index * capacity + row_rank // holders
    source_row = (
        jnp.full((wide_count * capacity,), row_count, jnp.int32).at[slot_index].set(positions)
    )
    whole = lax.all_gather(tokens, "narrow", axis=1, tiled=True)
    base_part = jnp.dot(whole, base_weight, preferred_element_type=jnp.float32)
    levels = delta_levels[0]
    scales = delta_scales[0]
    picked_cols = outlier_index[0]
    outlier_rows = outlier_values[0]
    outgoing = jnp.take(whole, source_row, axis=0, mode="fill", fill_value=0).reshape(
        wide_count, capacity, whole.shape[1]
    )
    received = lax.all_to_all(outgoing, "wide", split_axis=0, concat_axis=0, tiled=True)
    product = (
        jnp.einsum("nid,df->nif", received, levels, preferred_element_type=jnp.float32) * scales
    )
    chosen = jnp.take(received, picked_cols, axis=2)
    product = product + jnp.einsum(
        "nik,kf->nif", chosen, outlier_rows, preferred_element_type=jnp.float32
    )
    returned_rows = lax.all_to_all(
        product.astype(jnp.bfloat16), "wide", split_axis=0, concat_axis=0, tiled=True
    )
    update = jnp.take(
        returned_rows.reshape(wide_count * capacity, returned_rows.shape[2]), slot_index, axis=0
    )
    return (base_part + update.astype(jnp.float32)).astype(jnp.bfloat16)


def solution(mesh):
    placed = (
        P(("groups", "wide"), "narrow"),
        P("wide"),
        P(),
        P(None, "narrow"),
        P("wide", None, "narrow"),
        P("wide", "narrow"),
        P("wide", None),
        P("wide", None, "narrow"),
    )
    few = mesh.shape["wide"] == 4 and mesh.shape["narrow"] == 4 and mesh.shape["groups"] == 2
    return jax.shard_map(
        delta_plan if few else row_plan,
        mesh=mesh,
        in_specs=placed,
        out_specs=P(("groups", "wide"), "narrow"),
        check_vma=False,
    )
```
